128 devices in a mesh: gx: 16 (over z, y), gy: 8 (over x, core).
Axes of the slice: x: 4, y: 4, z: 4, core: 2. Of those that a mesh axis runs over, the one named last changes fastest.
Arguments:
- x_tokens: bfloat16 [4096, 1024], P(('gx', 'gy')), may hold values from -6 to 6
- dy_tokens: bfloat16 [1024, 16384], P(None, ('gx', 'gy')), may hold values from -0.03125 to 0.03125
- samples: int32 [256], replicated, may hold values from 0 to 1023
- grad_acc: float32 [4096, 16384], P(('gx', 'gy')), may hold values from -0.625 to 0.625
- owners: int32 [8, 32], replicated, may hold values from 0 to 7, as said below
- left_stats: float32 [128, 4, 512, 512], P(('gx', 'gy')), may hold values from -1 to 5
- right_stats: float32 [128, 4, 512, 512], P(('gx', 'gy')), may hold values from -1 to 5
- left_roots: bfloat16 [128, 4, 512, 512], P(('gx', 'gy')), may hold values from -1 to 3
- right_roots: bfloat16 [128, 4, 512, 512], P(('gx', 'gy')), may hold values from -1 to 3
Outputs:
- update: float32 [4096, 16384], P(('gx', 'gy'))
- new_left_stats: float32 [128, 4, 512, 512], P(('gx', 'gy'))
- new_right_stats: float32 [128, 4, 512, 512], P(('gx', 'gy'))
The draws below stay inside these ranges and needn't reach their ends.
Inputs may be any that keep to these rules, and one draw needn't show every extreme that they name: owners[r, c] is the gy index of the device that owns block (r, c) among the devices whose gx index is c // 2. The 2 blocks of one row r inside one column group have different owners; no device owns more than 4 blocks, and in every draw some device owns exactly 4. Slots past a device's count of blocks hold no block.
All inputs are finite; a program needn't handle non-finite values.
Results may differ from the reference program's by a relative error of at most 0.0041.
Values may be sent and summed in bfloat16 or wider, within the bound.
A program may use at most 128 MiB of HBM per device.

```python
import math
import jax
import jax.numpy as jnp
from jax import lax

BLK = 512
BCOL = 2
POOL = 1024
SAMPLES = 256
ROWS = 4096
COLS = 16384
SLOTS = 4


def definite(key, lowest, highest_value, coupling_scale):
    tile_count = ROWS // BLK
    matrix_count = tile_count * (COLS // (BLK * BCOL)) * SLOTS
    diagonal_key, coupling_key = jax.random.split(key)
    diagonal = jnp.exp(jax.random.uniform(diagonal_key, (matrix_count, BLK), jnp.float32, math.log(lowest), math.log(highest_value)))
    coupling = jnp.clip(jax.random.normal(coupling_key, (matrix_count, BLK, BLK), jnp.float32), -4.0, 4.0) * coupling_scale
    coupling = 0.5 * (coupling + jnp.swapaxes(coupling, 1, 2))
    identity = jnp.eye(BLK, dtype=jnp.float32)
    matrices = coupling + diagonal[:, :, None] * identity[None]
    return matrices.reshape(matrix_count // SLOTS, SLOTS, BLK, BLK)


def draw_left_stats(key, part):
    key = jax.random.fold_in(key, 3)
    return definite(key, 1.0, 4.0, 0.7 / math.sqrt(BLK))


def draw_right_stats(key, part):
    key = jax.random.fold_in(key, 5)
    return definite(key, 1.0, 4.0, 0.7 / math.sqrt(BLK))


def draw_left_roots(key, part):
    key = jax.random.fold_in(key, 7)
    return definite(key, 0.5, 2.0, 0.35 / math.sqrt(BLK)).astype(jnp.bfloat16)


def draw_right_roots(key, part):
    key = jax.random.fold_in(key, 9)
    return definite(key, 0.5, 2.0, 0.35 / math.sqrt(BLK)).astype(jnp.bfloat16)


def group_owners(tile_key, owner_key, paired):
    tile_count = ROWS // BLK
    tile_order = jax.random.permutation(tile_key, tile_count)
    owner_order = jax.random.permutation(owner_key, tile_count)
    first_owner = jnp.where(paired, tile_order // 2, tile_order)
    shifted = (first_owner[:, None] + jnp.arange(BCOL)[None, :]) % tile_count
    return owner_order[shifted]


def draw_owners(key, part):
    key = jax.random.fold_in(key, 11)
    tile_count = ROWS // BLK
    group_count = COLS // (BLK * BCOL)
    tile_keys = jax.random.split(jax.random.fold_in(key, 1), group_count)
    owner_keys = jax.random.split(jax.random.fold_in(key, 2), group_count)
    coin_flips = jax.random.randint(jax.random.fold_in(key, 3), (group_count,), 0, 2)
    forced = jax.random.randint(jax.random.fold_in(key, 4), (), 0, group_count)
    paired = (coin_flips == 1) | (jnp.arange(group_count) == forced)
    stacked = jax.vmap(group_owners)(tile_keys, owner_keys, paired)
    return stacked.transpose(1, 0, 2).reshape(tile_count, group_count * BCOL).astype(jnp.int32)


def with_ends(drawn, rng, low, largest):
    index_at = [jax.random.randint(jax.random.fold_in(rng, axis), (), 0, length) for axis, length in enumerate(drawn.shape)]
    widest = drawn.shape.index(max(drawn.shape))
    neighbour = index_at[:widest] + [(index_at[widest] + 1) % drawn.shape[widest]] + index_at[widest + 1:]
    return drawn.at[tuple(index_at)].set(low).at[tuple(neighbour)].set(largest)


def block_scale(stream_key, extent, shards, smallest, largest):
    def one(dim, shards_of):
        heights = jax.random.uniform(jax.random.fold_in(jax.random.fold_in(stream_key, 6), dim), (shards_of,), jnp.float32, smallest / len(shards), largest / len(shards))
        return jnp.repeat(jnp.exp(heights), extent[dim] // shards_of).reshape((-1,) + (1,) * (len(extent) - dim - 1))

    level = one(*shards[0])
    for cut in shards[1:]:
        level = level * one(*cut)
    return level


def noise(own_key, extent, deviation, reach, shards=(), kind=jnp.bfloat16):
    loudness = block_scale(own_key, extent, shards, -0.22, 0.18) if shards else 1.0
    array = jax.random.normal(own_key, extent, jnp.float32) * deviation * loudness
    return jnp.minimum(jnp.maximum(array, -reach), reach).astype(kind)


def setup_inputs(seed: int = 0) -> dict:
    key_list = jax.random.split(jax.random.key(seed), 10)
    return {
        "x_tokens": noise(key_list[0], (ROWS, POOL), 1.0, 6.0, ((0, 128),)),
        "dy_tokens": noise(key_list[1], (POOL, COLS), 0.006, 0.03125, ((1, 128),)),
        "samples": with_ends(jax.random.randint(key_list[2], (SAMPLES,), 0, POOL), jax.random.fold_in(key_list[2], 1), 0, POOL - 1).astype(jnp.int32),
        "grad_acc": noise(key_list[3], (ROWS, COLS), 0.1, 0.625, ((0, 128),), jnp.float32),
        "owners": draw_owners(jax.random.fold_in(key_list[9], 71), 0),
        "left_stats": draw_left_stats(jax.random.fold_in(key_list[9], 71), 0),
        "right_stats": draw_right_stats(jax.random.fold_in(key_list[9], 71), 0),
        "left_roots": draw_left_roots(jax.random.fold_in(key_list[9], 71), 0),
        "right_roots": draw_right_roots(jax.random.fold_in(key_list[9], 71), 0),
    }


BETA_TWO = 0.9
EPSILON = 1e-06

def block_step(grad_block, left_stat, right_stat, left_root, right_root):
    highest = lax.Precision.HIGHEST
    gram_left = jnp.dot(grad_block, grad_block.T, precision=highest, preferred_element_type=jnp.float32)
    gram_right = jnp.dot(grad_block.T, grad_block, precision=highest, preferred_element_type=jnp.float32)
    new_left = BETA_TWO * left_stat + (1.0 - BETA_TWO) * gram_left
    new_right = BETA_TWO * right_stat + (1.0 - BETA_TWO) * gram_right
    narrow = grad_block.astype(jnp.bfloat16)
    half_product = jnp.dot(left_root, narrow, preferred_element_type=jnp.float32).astype(jnp.bfloat16)
    direction = jnp.dot(half_product, right_root, preferred_element_type=jnp.float32)
    scaled = direction * lax.rsqrt(jnp.mean(direction * direction) + EPSILON)
    return (new_left, new_right, scaled)

def slot_ranks(listed):
    entry_count = listed.shape[-1]
    places = jnp.arange(entry_count)
    same_owner = listed[..., :, None] == listed[..., None, :]
    earlier = places[None, :] < places[:, None]
    return lax.optimization_barrier(jnp.sum(jnp.where(same_owner & earlier, 1, 0), axis=-1)).astype(jnp.int32)

def step_item(item_tuple):
    return block_step(item_tuple[0], item_tuple[1], item_tuple[2], item_tuple[3], item_tuple[4])

def reference(x_tokens, dy_tokens, samples, grad_acc, owners, left_stats, right_stats, left_roots, right_roots):
    highest = lax.Precision.HIGHEST
    row_count, col_count = grad_acc.shape
    block_rows = row_count // BLK
    block_cols = col_count // BLK
    groups = block_cols // BCOL
    picked_inputs = jnp.take(x_tokens, samples, axis=1).astype(jnp.float32)
    picked_cotangents = jnp.take(dy_tokens, samples, axis=0).astype(jnp.float32)
    gradient = grad_acc + jnp.dot(picked_inputs, picked_cotangents, precision=highest, preferred_element_type=jnp.float32)
    blocks = gradient.reshape(block_rows, BLK, block_cols, BLK).transpose(0, 2, 1, 3).reshape(block_rows * block_cols, BLK, BLK)
    grouped = owners.reshape(block_rows, groups, BCOL).transpose(1, 0, 2).reshape(groups, block_rows * BCOL)
    slot_rank = slot_ranks(grouped).reshape(groups, block_rows, BCOL).transpose(1, 0, 2).reshape(block_rows, block_cols)
    group_index = (jnp.arange(block_cols) // BCOL).astype(jnp.int32)
    device = group_index[None, :] * block_rows + owners.astype(jnp.int32)
    flat_slot = (device * SLOTS + slot_rank).reshape(-1).astype(jnp.int32)
    slot_total = left_stats.shape[0] * SLOTS
    left_flat = left_stats.reshape(slot_total, BLK, BLK)
    right_flat = right_stats.reshape(slot_total, BLK, BLK)
    lroot_flat = left_roots.reshape(slot_total, BLK, BLK)
    rroot_flat = right_roots.reshape(slot_total, BLK, BLK)
    gathered = (blocks, left_flat[flat_slot], right_flat[flat_slot], lroot_flat[flat_slot], rroot_flat[flat_slot])
    new_left, new_right, directions = lax.map(step_item, gathered)
    left_out = left_flat.at[flat_slot].set(new_left).reshape(left_stats.shape)
    right_out = right_flat.at[flat_slot].set(new_right).reshape(right_stats.shape)
    update = directions.reshape(block_rows, block_cols, BLK, BLK).transpose(0, 2, 1, 3).reshape(row_count, col_count)
    return (update, left_out, right_out)
```

```python
import functools

import jax
import jax.numpy as jnp
from jax import lax
from jax.experimental import pallas as pl
from jax.experimental.pallas import tpu as pltpu
from jax.sharding import PartitionSpec as P

BCOL = 2
SLOTS = 4
BETA_TWO = 0.9
EPSILON = 1e-06
CHUNKS = 4

MESH = pl.DeviceIdType.MESH
F32 = jnp.float32
BF16 = jnp.bfloat16


def exchange_kernel(
    nx, ny, q_count,
    x_ref, dy_ref, samples_ref, grad_ref, owners_ref, lroot_ref, rroot_ref,
    rows_out, grad_out,
    *scratch,
):
    names = iter(scratch)

    def several(count):
        return [next(names) for _ in range(count)]

    acc = several(q_count)
    mine = several(q_count)
    pack = several(q_count)
    held = several(q_count)
    send = several(q_count)
    back = several(q_count)
    strips = several(q_count)
    xs, dys, lroot, rroot, half, direction, source_tab, key_tab = several(8)
    (x_send, x_recv, dy_send, dy_recv, root_sem, keep_sem,
     a_send, a_recv, b_send, b_recv, c_send, c_recv, d_send, d_recv) = several(14)

    me_x, me_y = lax.axis_index("gx"), lax.axis_index("gy")
    fold = nx // ny
    rows = grad_ref.shape[0]
    blk = fold * ny * rows
    w = blk // q_count
    br = ny
    tile = BCOL * blk
    dcols = dy_ref.shape[1]
    entries = br * BCOL

    def peer_x(d):
        return lax.rem(me_x + d, nx)

    def peer_y(d):
        return lax.rem(me_y + d, ny)

    barrier = pltpu.get_barrier_semaphore()

    def greet_x(d, _):
        pl.semaphore_signal(barrier, inc=1, device_id=(peer_x(d), me_y), device_id_type=MESH)
        return 0

    def greet_y(d, _):
        pl.semaphore_signal(barrier, inc=1, device_id=(me_x, peer_y(d)), device_id_type=MESH)
        return 0

    lax.fori_loop(1, nx, greet_x, 0)
    lax.fori_loop(1, ny, greet_y, 0)

    roots = [
        pltpu.make_async_copy(lroot_ref, lroot, root_sem.at[0]),
        pltpu.make_async_copy(rroot_ref, rroot, root_sem.at[1]),
    ]
    for copy in roots:
        copy.start()
    pool = x_ref.shape[1]
    count = samples_ref.shape[1]
    chosen = (lax.broadcasted_iota(jnp.int32, (pool, count), 0) == samples_ref[...])
    chosen = jnp.where(chosen, 1.0, 0.0).astype(BF16)
    xs[pl.ds(me_x, 1)] = jnp.dot(x_ref[...], chosen, preferred_element_type=F32).astype(BF16)[None]
    my_cols = pl.ds(pl.multiple_of(me_y * dcols, dcols), dcols)
    dys[:, my_cols] = lax.dot_general(
        chosen, dy_ref[...], (((0,), (0,)), ((), ())), preferred_element_type=F32
    ).astype(BF16)

    pl.semaphore_wait(barrier, nx + ny - 2)

    def send_x(d, _):
        pltpu.make_async_remote_copy(
            xs.at[me_x], xs.at[me_x], x_send, x_recv, (peer_x(d), me_y), MESH
        ).start()
        return 0

    def send_dy(d, _):
        pltpu.make_async_remote_copy(
            dys.at[:, my_cols], dys.at[:, my_cols], dy_send, dy_recv, (me_x, peer_y(d)), MESH
        ).start()
        return 0

    def acc_source(group, block, q):
        first = pl.multiple_of(group * tile + block * blk + q * w, 128)
        return grad_ref.at[:, pl.ds(first, w)]

    lax.fori_loop(1, ny, send_dy, 0)
    lax.fori_loop(1, nx, send_x, 0)
    for q in range(q_count):
        for block in range(BCOL):
            pltpu.make_async_copy(
                acc_source(me_x, block, q), acc[q].at[me_x, block], a_recv.at[q]
            ).start()

        def send_acc(d, _, q=q):
            for block in range(BCOL):
                pltpu.make_async_remote_copy(
                    acc_source(peer_x(d), block, q), acc[q].at[me_x, block],
                    a_send.at[q], a_recv.at[q], (peer_x(d), me_y), MESH,
                ).start()
            return 0

        lax.fori_loop(1, nx, send_acc, 0)

    keys = []
    listed = [owners_ref[e // BCOL, me_x * BCOL + e % BCOL] for e in range(entries)]
    for e in range(entries):
        rank = jnp.int32(0)
        for before in range(e):
            rank = rank + jnp.where(listed[before] == listed[e], 1, 0)
        keys.append(listed[e] * SLOTS + rank)
        key_tab[e] = keys[e]

    def find_source(k, _):
        place = jnp.int32(0)
        for e in range(entries):
            place = place + jnp.where(keys[e] == k, (e % BCOL) * br + e // BCOL, 0)
        source_tab[k] = place
        return 0

    lax.fori_loop(0, ny * SLOTS, find_source, 0)

    def landed(ref, sem):
        pltpu.make_async_copy(ref, ref, sem).wait()

    for q in range(q_count):
        if q == 0:
            landed(xs.at[pl.ds(0, nx - 1)], x_recv)
            landed(dys.at[:, pl.ds(0, (ny - 1) * dcols)], dy_recv)
        landed(acc[q], a_recv.at[q])
        for block in range(BCOL):
            first = block * blk + q * w
            product = jnp.dot(
                xs[...].reshape(nx * rows, count), dys[:, first:first + w],
                preferred_element_type=F32,
            ).reshape(nx, rows, w)
            total = (acc[q][:, block] + product).astype(BF16)
            mine[q][block * br:(block + 1) * br] = total.reshape(br, fold, rows, w)

        def fill(owner, _, q=q):
            for slot in range(SLOTS):
                pack[q][owner, slot] = mine[q][source_tab[owner * SLOTS + slot]]
            return 0

        lax.fori_loop(0, ny, fill, 0)
        pltpu.make_async_copy(pack[q].at[me_y], held[q].at[:, :, me_y], b_recv.at[q]).start()

        def send_block(d, _, q=q):
            pltpu.make_async_remote_copy(
                pack[q].at[peer_y(d)], held[q].at[:, :, me_y],
                b_send.at[q], b_recv.at[q], (me_x, peer_y(d)), MESH,
            ).start()
            return 0

        lax.fori_loop(1, ny, send_block, 0)

    for copy in roots:
        copy.wait()

    kept = []
    for q in range(q_count):
        landed(held[q], b_recv.at[q])
        kept.append(pltpu.make_async_copy(
            held[q], grad_out.at[:, :, :, :, pl.ds(q * w, w)], keep_sem.at[q]
        ))
        kept[q].start()

        def left(slot, _, q=q):
            half[slot, :, q * w:(q + 1) * w] = jnp.dot(
                lroot[slot], held[q][slot].reshape(blk, w), preferred_element_type=F32
            ).astype(BF16)
            return 0

        lax.fori_loop(0, SLOTS, left, 0)

    part = blk // 4

    def right(slot, _):
        squares = jnp.zeros((1, blk), F32)
        for p in range(4):
            product = jnp.dot(
                half[slot, p * part:(p + 1) * part, :], rroot[slot], preferred_element_type=F32
            )
            direction[p * part:(p + 1) * part, :] = product
            squares = squares + jnp.sum(product * product, axis=0, keepdims=True)
        scale = lax.rsqrt(jnp.sum(squares) / (blk * blk) + EPSILON)
        for q in range(q_count):
            scaled = (direction[:, q * w:(q + 1) * w] * scale).astype(BF16)
            send[q][slot] = scaled.reshape(fold, ny, rows, w)
        return 0

    lax.fori_loop(0, SLOTS, right, 0)

    my_slots = pl.ds(me_y * SLOTS, SLOTS)
    for q in range(q_count):
        pltpu.make_async_copy(send[q].at[:, :, me_y], back[q].at[my_slots], c_recv.at[q]).start()

        def send_back(d, _, q=q):
            pltpu.make_async_remote_copy(
                send[q].at[:, :, peer_y(d)], back[q].at[my_slots],
                c_send.at[q], c_recv.at[q], (me_x, peer_y(d)), MESH,
            ).start()
            return 0

        lax.fori_loop(1, ny, send_back, 0)

    for q in range(q_count):
        landed(back[q], c_recv.at[q])
        for e in range(entries):
            r, block = e // BCOL, e % BCOL
            strips[q][r * fold:(r + 1) * fold, block] = back[q][key_tab[e]]
        pltpu.make_async_copy(strips[q].at[me_x], rows_out.at[q, me_x], d_recv.at[q]).start()

        def send_rows(d, _, q=q):
            pltpu.make_async_remote_copy(
                strips[q].at[peer_x(d)], rows_out.at[q, me_x],
                d_send.at[q], d_recv.at[q], (peer_x(d), me_y), MESH,
            ).start()
            return 0

        lax.fori_loop(1, nx, send_rows, 0)

    for q in range(q_count):
        landed(rows_out.at[q], d_recv.at[q])
        kept[q].wait()
        landed(acc[q].at[pl.ds(0, nx - 1)], a_send.at[q])
        landed(pack[q].at[pl.ds(0, ny - 1)], b_send.at[q])
        landed(pack[q].at[pl.ds(0, ny - 1)], c_send.at[q])
        landed(strips[q].at[pl.ds(0, nx - 1)], d_send.at[q])
    landed(xs.at[pl.ds(0, nx - 1)], x_send)
    landed(dys.at[:, pl.ds(0, (ny - 1) * dcols)], dy_send)


def finish_kernel(
    owners_ref, grad_ref, left_ref, right_ref, rows_ref, update_ref, new_left_ref, new_right_ref
):
    me_x, me_y = lax.axis_index("gx"), lax.axis_index("gy")
    slot, part = pl.program_id(0), pl.program_id(1)
    owned = jnp.int32(0)
    for r in range(owners_ref.shape[0]):
        for c in range(BCOL):
            owned = owned + jnp.where(owners_ref[r, me_x * BCOL + c] == me_y, 1, 0)
    occupied = slot < owned
    old = jnp.where(occupied, BETA_TWO, 1.0)
    new = jnp.where(occupied, 1.0 - BETA_TWO, 0.0)
    span = left_ref.shape[1]
    first = pl.multiple_of(part * span, span)
    block = grad_ref[0]
    gram_left = lax.dot_general(
        grad_ref[0, pl.ds(first, span), :], block, (((1,), (1,)), ((), ())), preferred_element_type=F32
    )
    new_left_ref[0] = old * left_ref[0] + new * gram_left
    gram_right = lax.dot_general(
        grad_ref[0, :, pl.ds(first, span)], block, (((0,), (0,)), ((), ())), preferred_element_type=F32
    )
    new_right_ref[0] = old * right_ref[0] + new * gram_right
    q_count, groups, blocks, _, w = rows_ref.shape
    for group in range(groups):
        for b in range(blocks):
            for q in range(q_count):
                at = ((group * blocks + b) * q_count + q) * w
                update_ref[:, at:at + w] = rows_ref[q, group, b].astype(F32)


def body(
    x_tokens, dy_tokens, samples, grad_acc, owners, left_stats, right_stats, left_roots, right_roots
):
    nx, ny = lax.axis_size("gx"), lax.axis_size("gy")
    rows, cols = grad_acc.shape
    fold = nx // ny
    blk = left_stats.shape[-1]
    q_count = CHUNKS
    w = blk // q_count
    count = samples.shape[0]
    br = ny
    dcols = dy_tokens.shape[1]
    vmem, hbm = pl.BlockSpec(memory_space=pltpu.VMEM), pl.BlockSpec(memory_space=pl.ANY)
    smem = pl.BlockSpec(memory_space=pltpu.SMEM)

    def each(shape, dtype):
        return [pltpu.VMEM(shape, dtype) for _ in range(q_count)]

    dma = pltpu.SemaphoreType.DMA
    rows_back, grad = pl.pallas_call(
        functools.partial(exchange_kernel, nx, ny, q_count),
        out_shape=(
            jax.ShapeDtypeStruct((q_count, nx, BCOL, rows, w), BF16),
            jax.ShapeDtypeStruct((SLOTS, fold, ny, rows, blk), BF16),
        ),
        in_specs=[vmem, vmem, vmem, hbm, smem, hbm, hbm],
        out_specs=(hbm, hbm),
        scratch_shapes=[
            *each((nx, BCOL, rows, w), F32),
            *each((BCOL * br, fold, rows, w), BF16),
            *each((ny, SLOTS, fold, rows, w), BF16),
            *each((SLOTS, fold, ny, rows, w), BF16),
            *each((SLOTS, fold, ny, rows, w), BF16),
            *each((ny * SLOTS, fold, rows, w), BF16),
            *each((nx, BCOL, rows, w), BF16),
            pltpu.VMEM((nx, rows, count), BF16),
            pltpu.VMEM((count, ny * dcols), BF16),
            pltpu.VMEM((SLOTS, blk, blk), BF16),
            pltpu.VMEM((SLOTS, blk, blk), BF16),
            pltpu.VMEM((SLOTS, blk, blk), BF16),
            pltpu.VMEM((blk, blk), F32),
            pltpu.SMEM((ny * SLOTS,), jnp.int32),
            pltpu.SMEM((br * BCOL,), jnp.int32),
            dma, dma, dma, dma, dma((2,)), dma((q_count,)),
            *[dma((q_count,)) for _ in range(8)],
        ],
        compiler_params=pltpu.CompilerParams(
            collective_id=0, has_side_effects=True, vmem_limit_bytes=48 * 2**20
        ),
        name="exchange",
    )(
        x_tokens, dy_tokens, samples.reshape(1, count), grad_acc, owners,
        left_roots[0], right_roots[0],
    )
    parts = 2
    span = blk // parts
    steps = SLOTS * parts
    tall = pl.BlockSpec((1, span, blk), lambda s, p: (s, p, 0))
    update, new_left, new_right = pl.pallas_call(
        finish_kernel,
        grid=(SLOTS, parts),
        out_shape=(
            jax.ShapeDtypeStruct((rows, cols), F32),
            jax.ShapeDtypeStruct((SLOTS, blk, blk), F32),
            jax.ShapeDtypeStruct((SLOTS, blk, blk), F32),
        ),
        in_specs=[
            smem,
            pl.BlockSpec((1, blk, blk), lambda s, p: (s, 0, 0)),
            tall,
            tall,
            pl.BlockSpec(
                (q_count, nx // steps, BCOL, rows, w), lambda s, p: (0, s * parts + p, 0, 0, 0)
            ),
        ],
        out_specs=(
            pl.BlockSpec((rows, cols // steps), lambda s, p: (0, s * parts + p)),
            tall,
            tall,
        ),
        compiler_params=pltpu.CompilerParams(vmem_limit_bytes=48 * 2**20),
        name="finish",
    )(owners, grad.reshape(SLOTS, blk, blk), left_stats[0], right_stats[0], rows_back)
    return update, new_left[None], new_right[None]


def solution(mesh):
    split = P(("gx", "gy"), None)
    deep = P(("gx", "gy"), None, None, None)
    return jax.shard_map(
        body,
        mesh=mesh,
        in_specs=(split, P(None, ("gx", "gy")), P(), split, P(), deep, deep, deep, deep),
        out_specs=(split, deep, deep),
        check_vma=False,
    )
```

```python
import functools

import jax
import jax.numpy as jnp
from jax import lax
from jax.experimental import pallas as pl
from jax.experimental.pallas import tpu as pltpu
from jax.sharding import PartitionSpec as P

BCOL = 2
SLOTS = 4
BETA_TWO = 0.9
EPSILON = 1e-06
CHUNKS = 4

MESH = pl.DeviceIdType.MESH
F32 = jnp.float32
BF16 = jnp.bfloat16


def exchange_kernel(
    nx, ny, q_count,
    x_hbm, dy_hbm, samples_hbm, grad_hbm, owners_hbm, left_hbm, right_hbm, lroot_hbm, rroot_hbm,
    rows_out, left_out, right_out,
    *scratch,
):
    names = iter(scratch)

    def several(count):
        return [next(names) for _ in range(count)]

    mine_rows = several(q_count)
    acc = several(q_count)
    mine = several(q_count)
    pack = several(q_count)
    send = several(q_count)
    back = several(q_count)
    strips = several(q_count)
    (held, xs, dys, lroot, rroot, half, direction, left, right,
     x_ref, dy_ref, samples_ref, grad_ref, owners_ref, source_tab, key_tab) = several(16)
    (in_sem, x_send, x_recv, dy_send, dy_recv, keep_sem,
     a_send, a_recv, b_send, b_recv, c_send, c_recv, d_send, d_recv) = several(14)

    me_x, me_y = lax.axis_index("gx"), lax.axis_index("gy")
    fold = nx // ny
    rows = grad_ref.shape[0]
    blk = fold * ny * rows
    w = blk // q_count
    br = ny
    tile = BCOL * blk
    dcols = dy_ref.shape[1]
    entries = br * BCOL

    def peer_x(d):
        return lax.rem(me_x + d, nx)

    def peer_y(d):
        return lax.rem(me_y + d, ny)

    barrier = pltpu.get_barrier_semaphore()

    def greet_x(d, _):
        pl.semaphore_signal(barrier, inc=1, device_id=(peer_x(d), me_y), device_id_type=MESH)
        return 0

    def greet_y(d, _):
        pl.semaphore_signal(barrier, inc=1, device_id=(me_x, peer_y(d)), device_id_type=MESH)
        return 0

    lax.fori_loop(1, nx, greet_x, 0)
    lax.fori_loop(1, ny, greet_y, 0)

    pairs = [
        (samples_hbm, samples_ref), (x_hbm, x_ref), (dy_hbm, dy_ref), (grad_hbm, grad_ref),
        (owners_hbm, owners_ref), (lroot_hbm, lroot), (rroot_hbm, rroot),
        (left_hbm, left), (right_hbm, right),
    ]
    loads = [pltpu.make_async_copy(a, b, in_sem.at[i]) for i, (a, b) in enumerate(pairs)]
    for load in loads:
        load.start()
    for load in loads[:3]:
        load.wait()
    pool = x_ref.shape[1]
    count = samples_ref.shape[1]
    chosen = (lax.broadcasted_iota(jnp.int32, (pool, count), 0) == samples_ref[...])
    chosen = jnp.where(chosen, 1.0, 0.0).astype(BF16)
    xs[pl.ds(me_x, 1)] = jnp.dot(x_ref[...], chosen, preferred_element_type=F32).astype(BF16)[None]
    my_cols = pl.ds(pl.multiple_of(me_y * dcols, dcols), dcols)
    dys[:, my_cols] = lax.dot_general(
        chosen, dy_ref[...], (((0,), (0,)), ((), ())), preferred_element_type=F32
    ).astype(BF16)
    loads[3].wait()

    def narrow(group, _):
        for q in range(q_count):
            for block in range(BCOL):
                first = pl.multiple_of(group * tile + block * blk + q * w, 128)
                mine_rows[q][group, block] = grad_ref[:, pl.ds(first, w)].astype(BF16)
        return 0

    lax.fori_loop(0, nx, narrow, 0)

    pl.semaphore_wait(barrier, nx + ny - 2)

    def send_x(d, _):
        pltpu.make_async_remote_copy(
            xs.at[me_x], xs.at[me_x], x_send, x_recv, (peer_x(d), me_y), MESH
        ).start()
        return 0

    def send_dy(d, _):
        pltpu.make_async_remote_copy(
            dys.at[:, my_cols], dys.at[:, my_cols], dy_send, dy_recv, (me_x, peer_y(d)), MESH
        ).start()
        return 0

    lax.fori_loop(1, ny, send_dy, 0)
    lax.fori_loop(1, nx, send_x, 0)
    for q in range(q_count):
        pltpu.make_async_copy(mine_rows[q].at[me_x], acc[q].at[me_x], a_recv.at[q]).start()

        def send_acc(d, _, q=q):
            pltpu.make_async_remote_copy(
                mine_rows[q].at[peer_x(d)], acc[q].at[me_x],
                a_send.at[q], a_recv.at[q], (peer_x(d), me_y), MESH,
            ).start()
            return 0

        lax.fori_loop(1, nx, send_acc, 0)

    loads[4].wait()
    keys = []
    owned = jnp.int32(0)
    listed = [owners_ref[e // BCOL, me_x * BCOL + e % BCOL] for e in range(entries)]
    for e in range(entries):
        rank = jnp.int32(0)
        for before in range(e):
            rank = rank + jnp.where(listed[before] == listed[e], 1, 0)
        keys.append(listed[e] * SLOTS + rank)
        key_tab[e] = keys[e]
        owned = owned + jnp.where(listed[e] == me_y, 1, 0)

    def find_source(k, _):
        place = jnp.int32(0)
        for e in range(entries):
            place = place + jnp.where(keys[e] == k, (e % BCOL) * br + e // BCOL, 0)
        source_tab[k] = place
        return 0

    lax.fori_loop(0, ny * SLOTS, find_source, 0)

    def landed(ref, sem):
        pltpu.make_async_copy(ref, ref, sem).wait()

    def chunk(q):
        return slice(q * w, (q + 1) * w)

    for q in range(q_count):
        if q == 0:
            landed(xs.at[pl.ds(0, nx - 1)], x_recv)
            landed(dys.at[:, pl.ds(0, (ny - 1) * dcols)], dy_recv)
        landed(acc[q], a_recv.at[q])
        for block in range(BCOL):
            first = block * blk + q * w
            product = jnp.dot(
                xs[...].reshape(nx * rows, count), dys[:, first:first + w],
                preferred_element_type=F32,
            ).reshape(nx, rows, w)
            total = (acc[q][:, block].astype(F32) + product).astype(BF16)
            mine[q][block * br:(block + 1) * br] = total.reshape(br, fold, rows, w)

        def fill(owner, _, q=q):
            for slot in range(SLOTS):
                pack[q][owner, slot] = mine[q][source_tab[owner * SLOTS + slot]]
            return 0

        lax.fori_loop(0, ny, fill, 0)
        spot = held.at[:, :, me_y, :, pl.ds(q * w, w)]
        pltpu.make_async_copy(pack[q].at[me_y], spot, b_recv.at[q]).start()

        def send_block(d, _, q=q, spot=spot):
            pltpu.make_async_remote_copy(
                pack[q].at[peer_y(d)], spot,
                b_send.at[q], b_recv.at[q], (me_x, peer_y(d)), MESH,
            ).start()
            return 0

        lax.fori_loop(1, ny, send_block, 0)

    loads[5].wait()
    loads[6].wait()

    for q in range(q_count):
        landed(held.at[:, :, :, :, pl.ds(q * w, w)], b_recv.at[q])

        def from_left(slot, _, q=q):
            half[slot, :, chunk(q)] = jnp.dot(
                lroot[slot], held[slot, :, :, :, chunk(q)].reshape(blk, w),
                preferred_element_type=F32,
            ).astype(BF16)
            return 0

        lax.fori_loop(0, SLOTS, from_left, 0)

    parts = 4
    part = blk // parts

    def from_right(slot, _):
        squares = jnp.zeros((1, blk), F32)
        for p in range(parts):
            product = jnp.dot(
                half[slot, p * part:(p + 1) * part, :], rroot[slot], preferred_element_type=F32
            )
            direction[p * part:(p + 1) * part, :] = product
            squares = squares + jnp.sum(product * product, axis=0, keepdims=True)
        scale = lax.rsqrt(jnp.sum(squares) / (blk * blk) + EPSILON)
        for q in range(q_count):
            scaled = (direction[:, chunk(q)] * scale).astype(BF16)
            send[q][slot] = scaled.reshape(fold, ny, rows, w)
        return 0

    lax.fori_loop(0, SLOTS, from_right, 0)

    my_slots = pl.ds(me_y * SLOTS, SLOTS)
    for q in range(q_count):
        pltpu.make_async_copy(send[q].at[:, :, me_y], back[q].at[my_slots], c_recv.at[q]).start()

        def send_back(d, _, q=q):
            pltpu.make_async_remote_copy(
                send[q].at[:, :, peer_y(d)], back[q].at[my_slots],
                c_send.at[q], c_recv.at[q], (me_x, peer_y(d)), MESH,
            ).start()
            return 0

        lax.fori_loop(1, ny, send_back, 0)

    loads[7].wait()
    loads[8].wait()

    def statistics(slot, _):
        occupied = slot < owned
        old = jnp.where(occupied, BETA_TWO, 1.0)
        new = jnp.where(occupied, 1.0 - BETA_TWO, 0.0)
        block = held[slot].reshape(blk, blk)
        for p in range(parts):
            at = slice(p * part, (p + 1) * part)
            strip = held[slot, p * fold // parts, (p * part // rows) % ny:][:part // rows].reshape(part, blk)
            gram = lax.dot_general(
                strip, block, (((1,), (1,)), ((), ())), preferred_element_type=F32
            )
            left[slot, at, :] = old * left[slot, at, :] + new * gram
            gram = lax.dot_general(
                held[slot, :, :, :, at].reshape(blk, part), block, (((0,), (0,)), ((), ())),
                preferred_element_type=F32,
            )
            right[slot, at, :] = old * right[slot, at, :] + new * gram
        return 0

    lax.fori_loop(0, SLOTS, statistics, 0)
    kept = [
        pltpu.make_async_copy(left, left_out, keep_sem.at[0]),
        pltpu.make_async_copy(right, right_out, keep_sem.at[1]),
    ]
    for copy in kept:
        copy.start()

    for q in range(q_count):
        landed(back[q], c_recv.at[q])
        for e in range(entries):
            r, block = e // BCOL, e % BCOL
            strips[q][r * fold:(r + 1) * fold, block] = back[q][key_tab[e]]
        pltpu.make_async_copy(strips[q].at[me_x], rows_out.at[q, me_x], d_recv.at[q]).start()

        def send_rows(d, _, q=q):
            pltpu.make_async_remote_copy(
                strips[q].at[peer_x(d)], rows_out.at[q, me_x],
                d_send.at[q], d_recv.at[q], (peer_x(d), me_y), MESH,
            ).start()
            return 0

        lax.fori_loop(1, nx, send_rows, 0)

    for q in range(q_count):
        landed(rows_out.at[q], d_recv.at[q])
        landed(acc[q].at[pl.ds(0, nx - 1)], a_send.at[q])
        landed(pack[q].at[pl.ds(0, ny - 1)], b_send.at[q])
        landed(pack[q].at[pl.ds(0, ny - 1)], c_send.at[q])
        landed(strips[q].at[pl.ds(0, nx - 1)], d_send.at[q])
    landed(xs.at[pl.ds(0, nx - 1)], x_send)
    landed(dys.at[:, pl.ds(0, (ny - 1) * dcols)], dy_send)
    for copy in kept:
        copy.wait()


def finish_kernel(rows_ref, left_ref, right_ref, update_out, left_out, right_out, wide, sems, out_sem):
    copies = [
        pltpu.make_async_copy(left_ref, left_out, sems.at[0]),
        pltpu.make_async_copy(right_ref, right_out, sems.at[1]),
    ]
    for copy in copies:
        copy.start()
    q_count, groups, blocks, _, w = rows_ref.shape
    span = blocks * q_count * w
    for group in range(groups):
        for b in range(blocks):
            for q in range(q_count):
                at = ((group * blocks + b) * q_count + q) * w
                wide[:, at:at + w] = rows_ref[q, group, b].astype(F32)
        at = pl.ds(group * span, span)
        copies.append(pltpu.make_async_copy(wide.at[:, at], update_out.at[:, at], out_sem.at[group]))
        copies[-1].start()
    for copy in copies:
        copy.wait()


def body(
    x_tokens, dy_tokens, samples, grad_acc, owners, left_stats, right_stats, left_roots, right_roots
):
    nx, ny = lax.axis_size("gx"), lax.axis_size("gy")
    rows, cols = grad_acc.shape
    fold = nx // ny
    blk = left_stats.shape[-1]
    q_count = CHUNKS
    w = blk // q_count
    count = samples.shape[0]
    br = ny
    dcols = dy_tokens.shape[1]
    vmem, hbm = pl.BlockSpec(memory_space=pltpu.VMEM), pl.BlockSpec(memory_space=pltpu.HBM)
    anywhere = pl.BlockSpec(memory_space=pl.ANY)

    def each(shape, dtype):
        return [pltpu.VMEM(shape, dtype) for _ in range(q_count)]

    dma = pltpu.SemaphoreType.DMA
    square = (SLOTS, blk, blk)
    rows_back, new_left, new_right = pl.pallas_call(
        functools.partial(exchange_kernel, nx, ny, q_count),
        out_shape=(
            pltpu.VMEM((q_count, nx, BCOL, rows, w), BF16),
            pltpu.VMEM(square, F32),
            pltpu.VMEM(square, F32),
        ),
        in_specs=[hbm] * 9,
        out_specs=(anywhere,) * 3,
        scratch_shapes=[
            *each((nx, BCOL, rows, w), BF16),
            *each((nx, BCOL, rows, w), BF16),
            *each((BCOL * br, fold, rows, w), BF16),
            *each((ny, SLOTS, fold, rows, w), BF16),
            *each((SLOTS, fold, ny, rows, w), BF16),
            *each((ny * SLOTS, fold, rows, w), BF16),
            *each((nx, BCOL, rows, w), BF16),
            pltpu.VMEM((SLOTS, fold, ny, rows, blk), BF16),
            pltpu.VMEM((nx, rows, count), BF16),
            pltpu.VMEM((count, ny * dcols), BF16),
            pltpu.VMEM(square, BF16),
            pltpu.VMEM(square, BF16),
            pltpu.VMEM(square, BF16),
            pltpu.VMEM((blk, blk), F32),
            pltpu.VMEM(square, F32),
            pltpu.VMEM(square, F32),
            pltpu.VMEM(x_tokens.shape, BF16),
            pltpu.VMEM(dy_tokens.shape, BF16),
            pltpu.VMEM((1, count), jnp.int32),
            pltpu.VMEM((rows, cols), F32),
            pltpu.SMEM(owners.shape, jnp.int32),
            pltpu.SMEM((ny * SLOTS,), jnp.int32),
            pltpu.SMEM((br * BCOL,), jnp.int32),
            dma((9,)), dma, dma, dma, dma, dma((2,)),
            *[dma((q_count,)) for _ in range(8)],
        ],
        compiler_params=pltpu.CompilerParams(
            collective_id=0, has_side_effects=True, vmem_limit_bytes=40 * 2**20
        ),
        name="exchange",
    )(*[
        pltpu.with_memory_space_constraint(array, pltpu.HBM)
        for array in (
            x_tokens, dy_tokens, samples.reshape(1, count), grad_acc, owners,
            left_stats[0], right_stats[0], left_roots[0], right_roots[0],
        )
    ])
    update, new_left, new_right = pl.pallas_call(
        finish_kernel,
        out_shape=(
            jax.ShapeDtypeStruct((rows, cols), F32),
            jax.ShapeDtypeStruct(square, F32),
            jax.ShapeDtypeStruct(square, F32),
        ),
        in_specs=[vmem, anywhere, anywhere],
        out_specs=(hbm,) * 3,
        scratch_shapes=[pltpu.VMEM((rows, cols), F32), dma((2,)), dma((nx,))],
        compiler_params=pltpu.CompilerParams(vmem_limit_bytes=16 * 2**20),
        name="finish",
    )(rows_back, new_left, new_right)
    return update, new_left[None], new_right[None]


def solution(mesh):
    split = P(("gx", "gy"), None)
    deep = P(("gx", "gy"), None, None, None)
    return jax.shard_map(
        body,
        mesh=mesh,
        in_specs=(split, P(None, ("gx", "gy")), P(), split, P(), deep, deep, deep, deep),
        out_specs=(split, deep, deep),
        check_vma=False,
    )
```

```python
import functools
import math

import jax
import jax.numpy as jnp
from jax import lax
from jax.experimental import pallas as pl
from jax.experimental.pallas import tpu as pltpu
from jax.sharding import PartitionSpec as P

BCOL = 2
SLOTS = 4
BETA_TWO = 0.9
EPSILON = 1e-06
COLUMNS = 4
FORWARD = ((0, 0, 1), (1, 0, 1), (2, 0, 1), (3, 0, 1))
LEAVE = (((0, 0),), ((0, 1), (1, 0)), ((0, 2),), ((0, 3), (1, 1), (1, 2), (1, 3)))
GROUPS = 2
BACKWARD = ((0, 0, 1), (1, 0, 1), (2, 0, 1), (3, 0, 2), (3, 1, 2))

MESH = pl.DeviceIdType.MESH
F32 = jnp.float32
BF16 = jnp.bfloat16


def cut(chunk, rows, w):
    column, part, parts = chunk
    height = rows // parts
    return column, height, pl.ds(part * height, height), pl.ds(column * w, w)


def exchange_kernel(
    nx, ny, columns, forward, backward,
    x_hbm, dy_hbm, samples_hbm, grad_hbm, owners_hbm, left_hbm, right_hbm, lroot_hbm, rroot_hbm,
    *scratch,
):
    names = iter(scratch)

    def several(count):
        return [next(names) for _ in range(count)]

    ahead, home = len(forward), len(backward)
    rows_out = several(home)
    left_out, right_out = several(2)
    mine_rows = several(ahead)
    acc = several(ahead)
    mine = several(ahead)
    pack = several(ahead)
    landing = several(ahead)
    send = several(home)
    back = several(home)
    strips = several(home)
    (held, xs, dys, lroot, rroot, half, direction, left, right,
     x_ref, dy_ref, samples_ref, grad_ref, owners_ref, source_tab, key_tab) = several(16)
    (ready, in_sem, x_send, x_recv, dy_send, dy_recv, keep_sem,
     a_send, a_recv, b_send, b_recv, c_send, c_recv, d_send, d_recv) = several(15)

    me_x, me_y = lax.axis_index("gx"), lax.axis_index("gy")
    fold = nx // ny
    rows = grad_ref.shape[0]
    blk = fold * ny * rows
    w = blk // columns
    br = ny
    tile = BCOL * blk
    dcols = dy_ref.shape[1]
    entries = br * BCOL
    span = SLOTS // GROUPS
    side = math.isqrt(nx)
    up, across = me_x // side, lax.rem(me_x, side)

    def peer_x(d, e):
        return lax.rem(up + d, side) * side + lax.rem(across + e, side)

    def peer_y(d):
        return lax.rem(me_y + d, ny)

    straight = [peer_x(*d) for n in range(1, side) for d in ((n, 0), (0, n))]
    diagonal = [peer_x(m, n) for m in range(1, side) for n in range(1, side)]
    others = [peer_y(n) for n in range(1, ny)]

    def for_straight(act):
        for gx in straight:
            act(gx)

    def for_diagonal(act):
        for gx in diagonal:
            act(gx)

    def for_y(act):
        for gy in others:
            act(gy)

    barrier = pltpu.get_barrier_semaphore()

    def greet(gx, gy):
        pl.semaphore_signal(barrier, inc=1, device_id=(gx, gy), device_id_type=MESH)

    for_straight(lambda gx: greet(gx, me_y))
    for_y(lambda gy: greet(me_x, gy))

    pairs = [
        (samples_hbm, samples_ref), (x_hbm, x_ref), (dy_hbm, dy_ref), (grad_hbm, grad_ref),
        (owners_hbm, owners_ref), (lroot_hbm, lroot), (rroot_hbm, rroot),
        (left_hbm, left), (right_hbm, right),
    ]
    loads = [pltpu.make_async_copy(a, b, in_sem.at[i]) for i, (a, b) in enumerate(pairs)]
    for load in loads[:5]:
        load.start()
    for load in loads[:3]:
        load.wait()
    pool = x_ref.shape[1]
    count = samples_ref.shape[1]
    chosen = (lax.broadcasted_iota(jnp.int32, (pool, count), 0) == samples_ref[...])
    chosen = jnp.where(chosen, 1.0, 0.0).astype(BF16)
    xs[pl.ds(me_x, 1)] = jnp.dot(x_ref[...], chosen, preferred_element_type=F32).astype(BF16)[None]
    dys[pl.ds(me_y, 1)] = lax.dot_general(
        chosen, dy_ref[...], (((0,), (0,)), ((), ())), preferred_element_type=F32
    ).astype(BF16)[None]
    loads[3].wait()

    def narrow(group, _):
        for i, chunk in enumerate(forward):
            column, _, its_rows, _ = cut(chunk, rows, w)
            for block in range(BCOL):
                first = pl.multiple_of(group * tile + block * blk + column * w, 128)
                mine_rows[i][group, block] = grad_ref[its_rows, pl.ds(first, w)].astype(BF16)
        return 0

    lax.fori_loop(0, nx, narrow, 0)

    def send_x(gx):
        pltpu.make_async_remote_copy(
            xs.at[me_x], xs.at[me_x], x_send, x_recv, (gx, me_y), MESH
        ).start()

    def send_dy(gy):
        pltpu.make_async_remote_copy(
            dys.at[me_y], dys.at[me_y], dy_send, dy_recv, (me_x, gy), MESH
        ).start()

    def send_acc(i):
        def act(gx):
            pltpu.make_async_remote_copy(
                mine_rows[i].at[gx], acc[i].at[me_x], a_send.at[i], a_recv.at[i], (gx, me_y), MESH
            ).start()

        return act

    def vouch(d, _):
        pl.semaphore_signal(ready, inc=1, device_id=(peer_x(0, d), me_y), device_id_type=MESH)
        return 0

    pl.semaphore_wait(barrier, 2 * (side - 1) + ny - 1)
    lax.fori_loop(1, side, vouch, 0)
    for_straight(send_x)
    for_y(send_dy)
    for_straight(send_acc(0))
    pl.semaphore_wait(ready, side - 1)
    for_diagonal(send_x)
    for_diagonal(send_acc(0))
    for i in range(ahead):
        pltpu.make_async_copy(mine_rows[i].at[me_x], acc[i].at[me_x], a_recv.at[i]).start()
        if i:
            for_straight(send_acc(i))
            for_diagonal(send_acc(i))

    for load in loads[5:]:
        load.start()

    loads[4].wait()
    keys = []
    owned = jnp.int32(0)
    listed = [owners_ref[e // BCOL, me_x * BCOL + e % BCOL] for e in range(entries)]
    for e in range(entries):
        rank = jnp.int32(0)
        for before in range(e):
            rank = rank + jnp.where(listed[before] == listed[e], 1, 0)
        keys.append(listed[e] * SLOTS + rank)
        key_tab[e] = keys[e]
        owned = owned + jnp.where(listed[e] == me_y, 1, 0)

    def find_source(k, _):
        place = jnp.int32(0)
        for e in range(entries):
            place = place + jnp.where(keys[e] == k, (e % BCOL) * br + e // BCOL, 0)
        source_tab[k] = place
        return 0

    lax.fori_loop(0, ny * SLOTS, find_source, 0)

    def landed(ref, sem):
        pltpu.make_async_copy(ref, ref, sem).wait()

    def picked(first):
        if dcols >= w:
            return dys[first // dcols, :, first % dcols:first % dcols + w]
        return jnp.concatenate([dys[j] for j in range(first // dcols, (first + w) // dcols)], axis=1)

    for i, chunk in enumerate(forward):
        column, height, its_rows, its_columns = cut(chunk, rows, w)
        if i == 0:
            landed(xs.at[pl.ds(0, nx - 1)], x_recv)
            landed(dys.at[pl.ds(0, ny - 1)], dy_recv)
        landed(acc[i], a_recv.at[i])
        for block in range(BCOL):
            product = jnp.dot(
                xs[:, its_rows, :].reshape(nx * height, count),
                picked(block * blk + column * w),
                preferred_element_type=F32,
            ).reshape(nx, height, w)
            total = (acc[i][:, block].astype(F32) + product).astype(BF16)
            mine[i][block * br:(block + 1) * br] = total.reshape(br, fold, height, w)

        def fill(owner, _, i=i):
            for slot in range(SLOTS):
                pack[i][owner, slot] = mine[i][source_tab[owner * SLOTS + slot]]
            return 0

        lax.fori_loop(0, ny, fill, 0)
        for group, k in LEAVE[i]:
            its_slots = pl.ds(group * span, span)
            spot = landing[k].at[me_y, its_slots]
            pltpu.make_async_copy(pack[k].at[me_y, its_slots], spot, b_recv.at[group, k]).start()

            def send_block(gy, group=group, k=k, spot=spot, its_slots=its_slots):
                pltpu.make_async_remote_copy(
                    pack[k].at[gy, its_slots], spot,
                    b_send.at[group, k], b_recv.at[group, k], (me_x, gy), MESH,
                ).start()

            for_y(send_block)

    loads[5].wait()
    loads[6].wait()

    parts = 4
    part = blk // parts
    bands = part // rows

    def from_right(slot, _):
        squares = jnp.zeros((1, blk), F32)
        for p in range(parts):
            product = jnp.dot(
                half[slot, p * part:(p + 1) * part, :], rroot[slot], preferred_element_type=F32
            )
            direction[p * part:(p + 1) * part, :] = product
            squares = squares + jnp.sum(product * product, axis=0, keepdims=True)
        scale = lax.rsqrt(jnp.sum(squares) / (blk * blk) + EPSILON)
        for i, chunk in enumerate(backward):
            column, height, its_rows, its_columns = cut(chunk, rows, w)
            begin = chunk[1] * height
            scaled = (direction[:, its_columns] * scale).astype(BF16).reshape(fold, ny, rows, w)
            for f in range(fold):
                send[i][:, slot, f] = scaled[f, :, begin:begin + height, :]
        return 0

    def statistics(slot, _):
        occupied = slot < owned
        old = jnp.where(occupied, BETA_TWO, 1.0)
        new = jnp.where(occupied, 1.0 - BETA_TWO, 0.0)
        block = held[slot].reshape(blk, blk)
        for p in range(parts):
            at = slice(p * part, (p + 1) * part)
            first = p * bands % ny
            strip = held[slot, p * bands // ny, first:first + bands].reshape(part, blk)
            gram = lax.dot_general(
                strip, block, (((1,), (1,)), ((), ())), preferred_element_type=F32
            )
            left[slot, at, :] = old * left[slot, at, :] + new * gram
            gram = lax.dot_general(
                held[slot, :, :, :, at].reshape(blk, part), block, (((0,), (0,)), ((), ())),
                preferred_element_type=F32,
            )
            right[slot, at, :] = old * right[slot, at, :] + new * gram
        return 0

    for group in range(GROUPS):
        first = group * span
        its_slots = pl.ds(first, span)
        for i, chunk in enumerate(forward):
            _, _, its_rows, its_columns = cut(chunk, rows, w)
            landed(landing[i].at[:, its_slots], b_recv.at[group, i])
            for slot in range(first, first + span):
                for f in range(fold):
                    held[slot, f, :, its_rows, its_columns] = landing[i][:, slot, f]

            def from_left(slot, _, its_columns=its_columns):
                half[slot, :, its_columns] = jnp.dot(
                    lroot[slot], held[slot, :, :, :, its_columns].reshape(blk, w),
                    preferred_element_type=F32,
                ).astype(BF16)
                return 0

            lax.fori_loop(first, first + span, from_left, 0)
        lax.fori_loop(first, first + span, from_right, 0)
        my_slots = pl.ds(me_y * SLOTS + first, span)
        for i in range(home):
            spot = back[i].at[my_slots]
            pltpu.make_async_copy(send[i].at[me_y, its_slots], spot, c_recv.at[group, i]).start()

            def send_back(gy, i=i, group=group, spot=spot, its_slots=its_slots):
                pltpu.make_async_remote_copy(
                    send[i].at[gy, its_slots], spot,
                    c_send.at[group, i], c_recv.at[group, i], (me_x, gy), MESH,
                ).start()

            for_y(send_back)

        if group == 0:
            loads[7].wait()
            loads[8].wait()
        lax.fori_loop(first, first + span, statistics, 0)

    kept = [
        pltpu.make_async_copy(left, left_out, keep_sem.at[0]),
        pltpu.make_async_copy(right, right_out, keep_sem.at[1]),
    ]
    for copy in kept:
        copy.start()

    def for_x(act):
        for_straight(act)
        for_diagonal(act)

    for i in range(home):
        for group in range(GROUPS):
            landed(back[i].at[pl.ds(0, ny * span)], c_recv.at[group, i])
        for e in range(entries):
            r, block = e // BCOL, e % BCOL
            strips[i][r * fold:(r + 1) * fold, block] = back[i][key_tab[e]]
        spot = rows_out[i].at[me_x]
        pltpu.make_async_copy(strips[i].at[me_x], spot, d_recv.at[i]).start()

        def send_rows(gx, i=i, spot=spot):
            pltpu.make_async_remote_copy(
                strips[i].at[gx], spot, d_send.at[i], d_recv.at[i], (gx, me_y), MESH
            ).start()

        for_x(send_rows)

    for i in range(home):
        landed(rows_out[i], d_recv.at[i])
    for i in range(ahead):
        landed(acc[i].at[pl.ds(0, nx - 1)], a_send.at[i])
        for group in range(GROUPS):
            landed(pack[i].at[pl.ds(0, ny - 1), pl.ds(0, span)], b_send.at[group, i])
    for i in range(home):
        for group in range(GROUPS):
            landed(back[i].at[pl.ds(0, (ny - 1) * span)], c_send.at[group, i])
        landed(strips[i].at[pl.ds(0, nx - 1)], d_send.at[i])
    landed(xs.at[pl.ds(0, nx - 1)], x_send)
    landed(dys.at[pl.ds(0, ny - 1)], dy_send)
    for copy in kept:
        copy.wait()


def finish_kernel(chunks, *refs):
    rows_refs = refs[:len(chunks)]
    left_ref, right_ref, update_out, left_out, right_out, wide, sems, out_sem = refs[len(chunks):]
    copies = [
        pltpu.make_async_copy(left_ref, left_out, sems.at[0]),
        pltpu.make_async_copy(right_ref, right_out, sems.at[1]),
    ]
    for copy in copies:
        copy.start()
    rows = wide.shape[0]
    groups, blocks, _, w = rows_refs[0].shape
    blk = wide.shape[1] // (groups * blocks)
    for group in range(groups):
        for b in range(blocks):
            for ref, chunk in zip(rows_refs, chunks):
                column, height, its_rows, _ = cut(chunk, rows, w)
                at = (group * blocks + b) * blk + column * w
                wide[its_rows, at:at + w] = ref[group, b].astype(F32)
        at = pl.ds(group * blocks * blk, blocks * blk)
        copies.append(pltpu.make_async_copy(wide.at[:, at], update_out.at[:, at], out_sem.at[group]))
        copies[-1].start()
    for copy in copies:
        copy.wait()


def body(
    x_tokens, dy_tokens, samples, grad_acc, owners, left_stats, right_stats, left_roots, right_roots
):
    nx, ny = lax.axis_size("gx"), lax.axis_size("gy")
    rows, cols = grad_acc.shape
    fold = nx // ny
    blk = left_stats.shape[-1]
    w = blk // COLUMNS
    count = samples.shape[0]
    br = ny
    dcols = dy_tokens.shape[1]
    vmem, hbm = pl.BlockSpec(memory_space=pltpu.VMEM), pl.BlockSpec(memory_space=pltpu.HBM)
    anywhere = pl.BlockSpec(memory_space=pl.ANY)

    def each(chunks, *shape):
        heights = [rows // chunk[2] for chunk in chunks]
        return [
            pltpu.VMEM(tuple(h if n is None else n for n in shape), BF16) for h in heights
        ]

    dma = pltpu.SemaphoreType.DMA
    square = (SLOTS, blk, blk)
    *rows_back, new_left, new_right = pl.pallas_call(
        functools.partial(exchange_kernel, nx, ny, COLUMNS, FORWARD, BACKWARD),
        out_shape=(
            *each(BACKWARD, nx, BCOL, None, w),
            pltpu.VMEM(square, F32),
            pltpu.VMEM(square, F32),
        ),
        in_specs=[hbm] * 9,
        out_specs=(anywhere,) * (len(BACKWARD) + 2),
        scratch_shapes=[
            *each(FORWARD, nx, BCOL, None, w),
            *each(FORWARD, nx, BCOL, None, w),
            *each(FORWARD, BCOL * br, fold, None, w),
            *each(FORWARD, ny, SLOTS, fold, None, w),
            *each(FORWARD, ny, SLOTS, fold, None, w),
            *each(BACKWARD, ny, SLOTS, fold, None, w),
            *each(BACKWARD, ny * SLOTS, fold, None, w),
            *each(BACKWARD, nx, BCOL, None, w),
            pltpu.VMEM((SLOTS, fold, ny, rows, blk), BF16),
            pltpu.VMEM((nx, rows, count), BF16),
            pltpu.VMEM((ny, count, dcols), BF16),
            pltpu.VMEM(square, BF16),
            pltpu.VMEM(square, BF16),
            pltpu.VMEM(square, BF16),
            pltpu.VMEM((blk, blk), F32),
            pltpu.VMEM(square, F32),
            pltpu.VMEM(square, F32),
            pltpu.VMEM(x_tokens.shape, BF16),
            pltpu.VMEM(dy_tokens.shape, BF16),
            pltpu.VMEM((1, count), jnp.int32),
            pltpu.VMEM((rows, cols), F32),
            pltpu.SMEM(owners.shape, jnp.int32),
            pltpu.SMEM((ny * SLOTS,), jnp.int32),
            pltpu.SMEM((br * BCOL,), jnp.int32),
            pltpu.SemaphoreType.REGULAR,
            dma((9,)), *[dma] * 4, dma((2,)),
            *[dma((len(FORWARD),))] * 2,
            *[dma((GROUPS, len(FORWARD)))] * 2,
            *[dma((GROUPS, len(BACKWARD)))] * 2,
            *[dma((len(BACKWARD),))] * 2,
        ],
        compiler_params=pltpu.CompilerParams(
            collective_id=0, has_side_effects=True, vmem_limit_bytes=42 * 2**20
        ),
        name="exchange",
    )(*[
        pltpu.with_memory_space_constraint(array, pltpu.HBM)
        for array in (
            x_tokens, dy_tokens, samples.reshape(1, count), grad_acc, owners,
            left_stats[0], right_stats[0], left_roots[0], right_roots[0],
        )
    ])
    update, new_left, new_right = pl.pallas_call(
        functools.partial(finish_kernel, BACKWARD),
        out_shape=(
            jax.ShapeDtypeStruct((rows, cols), F32),
            jax.ShapeDtypeStruct(square, F32),
            jax.ShapeDtypeStruct(square, F32),
        ),
        in_specs=[vmem] * len(BACKWARD) + [anywhere] * 2,
        out_specs=(hbm,) * 3,
        scratch_shapes=[pltpu.VMEM((rows, cols), F32), dma((2,)), dma((nx,))],
        compiler_params=pltpu.CompilerParams(vmem_limit_bytes=12 * 2**20),
        name="finish",
    )(*rows_back, new_left, new_right)
    return update, new_left[None], new_right[None]


def solution(mesh):
    split = P(("gx", "gy"), None)
    deep = P(("gx", "gy"), None, None, None)
    return jax.shard_map(
        body,
        mesh=mesh,
        in_specs=(split, P(None, ("gx", "gy")), P(), split, P(), deep, deep, deep, deep),
        out_specs=(split, deep, deep),
        check_vma=False,
    )
```

```python
import functools
import math

import jax
import jax.numpy as jnp
from jax import lax
from jax.experimental import pallas as pl
from jax.experimental.pallas import tpu as pltpu
from jax.sharding import PartitionSpec as P

BCOL = 2
SLOTS = 4
BETA_TWO = 0.9
EPSILON = 1e-06
COLUMNS = 4
FORWARD = ((0, 0, 1), (1, 0, 1), (2, 0, 1), (3, 0, 1))
LEAVE = (((0, 0), (1, 0)), ((0, 1),), ((0, 2),), ((0, 3), (1, 1), (1, 2), (1, 3)))
GROUPS = 2
FIRST = 3
BACKWARD = ((0, 0, 1), (1, 0, 1), (2, 0, 1), (3, 0, 2), (3, 1, 2))

MESH = pl.DeviceIdType.MESH
F32 = jnp.float32
BF16 = jnp.bfloat16


def cut(chunk, rows, w):
    column, part, parts = chunk
    height = rows // parts
    return column, height, pl.ds(part * height, height), pl.ds(column * w, w)


def exchange_kernel(
    nx, ny, columns, forward, backward,
    x_hbm, dy_hbm, samples_hbm, grad_hbm, owners_hbm, left_hbm, right_hbm, lroot_hbm, rroot_hbm,
    *scratch,
):
    names = iter(scratch)

    def several(count):
        return [next(names) for _ in range(count)]

    ahead, home = len(forward), len(backward)
    rows_out = several(home)
    left_out, right_out = several(2)
    mine_rows = several(ahead)
    acc = several(ahead)
    mine = several(ahead)
    pack = several(ahead)
    landing = several(ahead)
    send = several(home)
    back = several(home)
    strips = several(home)
    (held, xs, dys, lroot, rroot, half, direction, left, right,
     x_ref, dy_ref, samples_ref, grad_ref, owners_ref, source_tab, key_tab) = several(16)
    (ready, in_sem, x_send, x_recv, dy_send, dy_recv, keep_sem,
     a_send, a_recv, b_send, b_recv, c_send, c_recv, d_send, d_recv) = several(15)

    me_x, me_y = lax.axis_index("gx"), lax.axis_index("gy")
    fold = nx // ny
    rows = grad_ref.shape[0]
    blk = fold * ny * rows
    w = blk // columns
    br = ny
    tile = BCOL * blk
    dcols = dy_ref.shape[1]
    entries = br * BCOL
    span = SLOTS // GROUPS
    side = math.isqrt(nx)
    up, across = me_x // side, lax.rem(me_x, side)

    def peer_x(d, e):
        return lax.rem(up + d, side) * side + lax.rem(across + e, side)

    def peer_y(d):
        return lax.rem(me_y + d, ny)

    straight = [peer_x(*d) for n in range(1, side) for d in ((n, 0), (0, n))]
    diagonal = [peer_x(m, n) for m in range(1, side) for n in range(1, side)]
    others = [peer_y(n) for n in range(1, ny)]

    def for_straight(act):
        for gx in straight:
            act(gx)

    def for_diagonal(act):
        for gx in diagonal:
            act(gx)

    def for_y(act):
        for gy in others:
            act(gy)

    barrier = pltpu.get_barrier_semaphore()

    def greet(gx, gy):
        pl.semaphore_signal(barrier, inc=1, device_id=(gx, gy), device_id_type=MESH)

    for_straight(lambda gx: greet(gx, me_y))
    for_y(lambda gy: greet(me_x, gy))

    pairs = [
        (samples_hbm, samples_ref), (x_hbm, x_ref), (dy_hbm, dy_ref), (grad_hbm, grad_ref),
        (owners_hbm, owners_ref), (lroot_hbm, lroot), (rroot_hbm, rroot),
        (left_hbm, left), (right_hbm, right),
    ]
    loads = [pltpu.make_async_copy(a, b, in_sem.at[i]) for i, (a, b) in enumerate(pairs)]
    for load in loads[:5]:
        load.start()
    for load in loads[:3]:
        load.wait()
    pool = x_ref.shape[1]
    count = samples_ref.shape[1]
    chosen = (lax.broadcasted_iota(jnp.int32, (pool, count), 0) == samples_ref[...])
    chosen = jnp.where(chosen, 1.0, 0.0).astype(BF16)
    xs[pl.ds(me_x, 1)] = jnp.dot(x_ref[...], chosen, preferred_element_type=F32).astype(BF16)[None]
    dys[pl.ds(me_y, 1)] = lax.dot_general(
        chosen, dy_ref[...], (((0,), (0,)), ((), ())), preferred_element_type=F32
    ).astype(BF16)[None]
    loads[3].wait()

    def narrow(group, _):
        for i, chunk in enumerate(forward):
            column, _, its_rows, _ = cut(chunk, rows, w)
            for block in range(BCOL):
                first = pl.multiple_of(group * tile + block * blk + column * w, 128)
                mine_rows[i][group, block] = grad_ref[its_rows, pl.ds(first, w)].astype(BF16)
        return 0

    lax.fori_loop(0, nx, narrow, 0)

    def send_x(gx):
        pltpu.make_async_remote_copy(
            xs.at[me_x], xs.at[me_x], x_send, x_recv, (gx, me_y), MESH
        ).start()

    def send_dy(gy):
        pltpu.make_async_remote_copy(
            dys.at[me_y], dys.at[me_y], dy_send, dy_recv, (me_x, gy), MESH
        ).start()

    def send_acc(i):
        def act(gx):
            pltpu.make_async_remote_copy(
                mine_rows[i].at[gx], acc[i].at[me_x], a_send.at[i], a_recv.at[i], (gx, me_y), MESH
            ).start()

        return act

    def vouch(d, _):
        pl.semaphore_signal(ready, inc=1, device_id=(peer_x(0, d), me_y), device_id_type=MESH)
        return 0

    pl.semaphore_wait(barrier, 2 * (side - 1) + ny - 1)
    lax.fori_loop(1, side, vouch, 0)
    for_straight(send_x)
    for_y(send_dy)
    for_straight(send_acc(0))
    pl.semaphore_wait(ready, side - 1)
    for_diagonal(send_x)
    for_diagonal(send_acc(0))
    for i in range(ahead):
        pltpu.make_async_copy(mine_rows[i].at[me_x], acc[i].at[me_x], a_recv.at[i]).start()
        if i:
            for_straight(send_acc(i))
            for_diagonal(send_acc(i))

    for load in loads[5:]:
        load.start()

    loads[4].wait()
    keys = []
    owned = jnp.int32(0)
    listed = [owners_ref[e // BCOL, me_x * BCOL + e % BCOL] for e in range(entries)]
    for e in range(entries):
        rank = jnp.int32(0)
        for before in range(e):
            rank = rank + jnp.where(listed[before] == listed[e], 1, 0)
        keys.append(listed[e] * SLOTS + rank)
        key_tab[e] = keys[e]
        owned = owned + jnp.where(listed[e] == me_y, 1, 0)

    def find_source(k, _):
        place = jnp.int32(0)
        for e in range(entries):
            place = place + jnp.where(keys[e] == k, (e % BCOL) * br + e // BCOL, 0)
        source_tab[k] = place
        return 0

    lax.fori_loop(0, ny * SLOTS, find_source, 0)

    def landed(ref, sem):
        pltpu.make_async_copy(ref, ref, sem).wait()

    def picked(first):
        if dcols >= w:
            return dys[first // dcols, :, first % dcols:first % dcols + w]
        return jnp.concatenate([dys[j] for j in range(first // dcols, (first + w) // dcols)], axis=1)

    for i, chunk in enumerate(forward):
        column, height, its_rows, its_columns = cut(chunk, rows, w)
        if i == 0:
            landed(xs.at[pl.ds(0, nx - 1)], x_recv)
            landed(dys.at[pl.ds(0, ny - 1)], dy_recv)
        landed(acc[i], a_recv.at[i])
        for block in range(BCOL):
            product = jnp.dot(
                xs[:, its_rows, :].reshape(nx * height, count),
                picked(block * blk + column * w),
                preferred_element_type=F32,
            ).reshape(nx, height, w)
            total = (acc[i][:, block].astype(F32) + product).astype(BF16)
            mine[i][block * br:(block + 1) * br] = total.reshape(br, fold, height, w)

        def fill(owner, _, i=i):
            for slot in range(SLOTS):
                pack[i][owner, slot] = mine[i][source_tab[owner * SLOTS + slot]]
            return 0

        lax.fori_loop(0, ny, fill, 0)
        for group, k in LEAVE[i]:
            its_slots = pl.ds(group * span, span)
            spot = landing[k].at[me_y, its_slots]
            pltpu.make_async_copy(pack[k].at[me_y, its_slots], spot, b_recv.at[group, k]).start()

            def send_block(gy, group=group, k=k, spot=spot, its_slots=its_slots):
                pltpu.make_async_remote_copy(
                    pack[k].at[gy, its_slots], spot,
                    b_send.at[group, k], b_recv.at[group, k], (me_x, gy), MESH,
                ).start()

            for_y(send_block)

    loads[5].wait()
    loads[6].wait()

    parts = 4
    part = blk // parts
    bands = part // rows

    def from_right(slot, _):
        squares = jnp.zeros((1, blk), F32)
        for p in range(parts):
            product = jnp.dot(
                half[slot, p * part:(p + 1) * part, :], rroot[slot], preferred_element_type=F32
            )
            direction[p * part:(p + 1) * part, :] = product
            squares = squares + jnp.sum(product * product, axis=0, keepdims=True)
        scale = lax.rsqrt(jnp.sum(squares) / (blk * blk) + EPSILON)
        for i, chunk in enumerate(backward):
            column, height, its_rows, its_columns = cut(chunk, rows, w)
            begin = chunk[1] * height
            scaled = (direction[:, its_columns] * scale).astype(BF16).reshape(fold, ny, rows, w)
            for f in range(fold):
                send[i][:, slot, f] = scaled[f, :, begin:begin + height, :]
        return 0

    def statistics(slot, _):
        occupied = slot < owned
        old = jnp.where(occupied, BETA_TWO, 1.0)
        new = jnp.where(occupied, 1.0 - BETA_TWO, 0.0)
        block = held[slot].reshape(blk, blk)
        for p in range(parts):
            at = slice(p * part, (p + 1) * part)
            first = p * bands % ny
            strip = held[slot, p * bands // ny, first:first + bands].reshape(part, blk)
            gram = lax.dot_general(
                strip, block, (((1,), (1,)), ((), ())), preferred_element_type=F32
            )
            left[slot, at, :] = old * left[slot, at, :] + new * gram
            gram = lax.dot_general(
                held[slot, :, :, :, at].reshape(blk, part), block, (((0,), (0,)), ((), ())),
                preferred_element_type=F32,
            )
            right[slot, at, :] = old * right[slot, at, :] + new * gram
        return 0

    def send_back(group, i):
        its_slots = pl.ds(group * span, span)
        spot = back[i].at[pl.ds(me_y * SLOTS + group * span, span)]
        pltpu.make_async_copy(send[i].at[me_y, its_slots], spot, c_recv.at[group, i]).start()

        def act(gy):
            pltpu.make_async_remote_copy(
                send[i].at[gy, its_slots], spot,
                c_send.at[group, i], c_recv.at[group, i], (me_x, gy), MESH,
            ).start()

        for_y(act)

    def sent_back(group, i):
        landed(back[i].at[pl.ds(0, (ny - 1) * span)], c_send.at[group, i])

    for group in range(GROUPS):
        first = group * span
        its_slots = pl.ds(first, span)
        for i, chunk in enumerate(forward):
            _, _, its_rows, its_columns = cut(chunk, rows, w)
            landed(landing[i].at[:, its_slots], b_recv.at[group, i])
            for slot in range(first, first + span):
                for f in range(fold):
                    held[slot, f, :, its_rows, its_columns] = landing[i][:, slot, f]

            def from_left(slot, _, its_columns=its_columns):
                half[slot, :, its_columns] = jnp.dot(
                    lroot[slot], held[slot, :, :, :, its_columns].reshape(blk, w),
                    preferred_element_type=F32,
                ).astype(BF16)
                return 0

            lax.fori_loop(first, first + span, from_left, 0)
        lax.fori_loop(first, first + span, from_right, 0)
        for i in range(FIRST):
            send_back(group, i)
        if group == 0:
            loads[7].wait()
            loads[8].wait()
        lax.fori_loop(first, first + span, statistics, 0)

    for i in range(FIRST, home):
        for group in range(GROUPS):
            send_back(group, i)
    kept = [
        pltpu.make_async_copy(left, left_out, keep_sem.at[0]),
        pltpu.make_async_copy(right, right_out, keep_sem.at[1]),
    ]
    for copy in kept:
        copy.start()

    def for_x(act):
        for_straight(act)
        for_diagonal(act)

    for i in range(home):
        for group in range(GROUPS):
            landed(back[i].at[pl.ds(0, ny * span)], c_recv.at[group, i])
        for e in range(entries):
            r, block = e // BCOL, e % BCOL
            strips[i][r * fold:(r + 1) * fold, block] = back[i][key_tab[e]]
        spot = rows_out[i].at[me_x]
        pltpu.make_async_copy(strips[i].at[me_x], spot, d_recv.at[i]).start()

        def send_rows(gx, i=i, spot=spot):
            pltpu.make_async_remote_copy(
                strips[i].at[gx], spot, d_send.at[i], d_recv.at[i], (gx, me_y), MESH
            ).start()

        for_x(send_rows)

    for i in range(home):
        landed(rows_out[i], d_recv.at[i])
    for i in range(ahead):
        landed(acc[i].at[pl.ds(0, nx - 1)], a_send.at[i])
        for group in range(GROUPS):
            landed(pack[i].at[pl.ds(0, ny - 1), pl.ds(0, span)], b_send.at[group, i])
    for i in range(home):
        for group in range(GROUPS):
            sent_back(group, i)
        landed(strips[i].at[pl.ds(0, nx - 1)], d_send.at[i])
    landed(xs.at[pl.ds(0, nx - 1)], x_send)
    landed(dys.at[pl.ds(0, ny - 1)], dy_send)
    for copy in kept:
        copy.wait()


def finish_kernel(chunks, *refs):
    rows_refs = refs[:len(chunks)]
    left_ref, right_ref, update_out, left_out, right_out, wide, sems, out_sem = refs[len(chunks):]
    copies = [
        pltpu.make_async_copy(left_ref, left_out, sems.at[0]),
        pltpu.make_async_copy(right_ref, right_out, sems.at[1]),
    ]
    for copy in copies:
        copy.start()
    rows = wide.shape[0]
    groups, blocks, _, w = rows_refs[0].shape
    blk = wide.shape[1] // (groups * blocks)
    for group in range(groups):
        for b in range(blocks):
            for ref, chunk in zip(rows_refs, chunks):
                column, height, its_rows, _ = cut(chunk, rows, w)
                at = (group * blocks + b) * blk + column * w
                wide[its_rows, at:at + w] = ref[group, b].astype(F32)
        at = pl.ds(group * blocks * blk, blocks * blk)
        copies.append(pltpu.make_async_copy(wide.at[:, at], update_out.at[:, at], out_sem.at[group]))
        copies[-1].start()
    for copy in copies:
        copy.wait()


def body(
    x_tokens, dy_tokens, samples, grad_acc, owners, left_stats, right_stats, left_roots, right_roots
):
    nx, ny = lax.axis_size("gx"), lax.axis_size("gy")
    rows, cols = grad_acc.shape
    fold = nx // ny
    blk = left_stats.shape[-1]
    w = blk // COLUMNS
    count = samples.shape[0]
    br = ny
    dcols = dy_tokens.shape[1]
    vmem, hbm = pl.BlockSpec(memory_space=pltpu.VMEM), pl.BlockSpec(memory_space=pltpu.HBM)
    anywhere = pl.BlockSpec(memory_space=pl.ANY)

    def each(chunks, *shape):
        heights = [rows // chunk[2] for chunk in chunks]
        return [
            pltpu.VMEM(tuple(h if n is None else n for n in shape), BF16) for h in heights
        ]

    dma = pltpu.SemaphoreType.DMA
    square = (SLOTS, blk, blk)
    *rows_back, new_left, new_right = pl.pallas_call(
        functools.partial(exchange_kernel, nx, ny, COLUMNS, FORWARD, BACKWARD),
        out_shape=(
            *each(BACKWARD, nx, BCOL, None, w),
            pltpu.VMEM(square, F32),
            pltpu.VMEM(square, F32),
        ),
        in_specs=[hbm] * 9,
        out_specs=(anywhere,) * (len(BACKWARD) + 2),
        scratch_shapes=[
            *each(FORWARD, nx, BCOL, None, w),
            *each(FORWARD, nx, BCOL, None, w),
            *each(FORWARD, BCOL * br, fold, None, w),
            *each(FORWARD, ny, SLOTS, fold, None, w),
            *each(FORWARD, ny, SLOTS, fold, None, w),
            *each(BACKWARD, ny, SLOTS, fold, None, w),
            *each(BACKWARD, ny * SLOTS, fold, None, w),
            *each(BACKWARD, nx, BCOL, None, w),
            pltpu.VMEM((SLOTS, fold, ny, rows, blk), BF16),
            pltpu.VMEM((nx, rows, count), BF16),
            pltpu.VMEM((ny, count, dcols), BF16),
            pltpu.VMEM(square, BF16),
            pltpu.VMEM(square, BF16),
            pltpu.VMEM(square, BF16),
            pltpu.VMEM((blk, blk), F32),
            pltpu.VMEM(square, F32),
            pltpu.VMEM(square, F32),
            pltpu.VMEM(x_tokens.shape, BF16),
            pltpu.VMEM(dy_tokens.shape, BF16),
            pltpu.VMEM((1, count), jnp.int32),
            pltpu.VMEM((rows, cols), F32),
            pltpu.SMEM(owners.shape, jnp.int32),
            pltpu.SMEM((ny * SLOTS,), jnp.int32),
            pltpu.SMEM((br * BCOL,), jnp.int32),
            pltpu.SemaphoreType.REGULAR,
            dma((9,)), *[dma] * 4, dma((2,)),
            *[dma((len(FORWARD),))] * 2,
            *[dma((GROUPS, len(FORWARD)))] * 2,
            *[dma((GROUPS, len(BACKWARD)))] * 2,
            *[dma((len(BACKWARD),))] * 2,
        ],
        compiler_params=pltpu.CompilerParams(
            collective_id=0, has_side_effects=True, vmem_limit_bytes=42 * 2**20
        ),
        name="exchange",
    )(*[
        pltpu.with_memory_space_constraint(array, pltpu.HBM)
        for array in (
            x_tokens, dy_tokens, samples.reshape(1, count), grad_acc, owners,
            left_stats[0], right_stats[0], left_roots[0], right_roots[0],
        )
    ])
    update, new_left, new_right = pl.pallas_call(
        functools.partial(finish_kernel, BACKWARD),
        out_shape=(
            jax.ShapeDtypeStruct((rows, cols), F32),
            jax.ShapeDtypeStruct(square, F32),
            jax.ShapeDtypeStruct(square, F32),
        ),
        in_specs=[vmem] * len(BACKWARD) + [anywhere] * 2,
        out_specs=(hbm,) * 3,
        scratch_shapes=[pltpu.VMEM((rows, cols), F32), dma((2,)), dma((nx,))],
        compiler_params=pltpu.CompilerParams(vmem_limit_bytes=12 * 2**20),
        name="finish",
    )(*rows_back, new_left, new_right)
    return update, new_left[None], new_right[None]


def solution(mesh):
    split = P(("gx", "gy"), None)
    deep = P(("gx", "gy"), None, None, None)
    return jax.shard_map(
        body,
        mesh=mesh,
        in_specs=(split, P(None, ("gx", "gy")), P(), split, P(), deep, deep, deep, deep),
        out_specs=(split, deep, deep),
        check_vma=False,
    )
```

```python
import functools
import math

import jax
import jax.numpy as jnp
from jax import lax
from jax.experimental import pallas as pl
from jax.experimental.pallas import tpu as pltpu
from jax.sharding import PartitionSpec as P

BCOL = 2
SLOTS = 4
BETA_TWO = 0.9
EPSILON = 1e-06
COLUMNS = 4
FORWARD = ((0, 0, 1), (1, 0, 1), (2, 0, 1), (3, 0, 1))
LEAVE = (((0, 0), (1, 0)), ((0, 1),), ((0, 2),), ((0, 3), (1, 1), (1, 2), (1, 3)))
GROUPS = 2
FIRST = 5
BACKWARD = tuple((column, part, 2) for column in range(COLUMNS) for part in range(2))

MESH = pl.DeviceIdType.MESH
F32 = jnp.float32
BF16 = jnp.bfloat16


def cut(chunk, rows, w):
    column, part, parts = chunk
    height = rows // parts
    return column, height, pl.ds(part * height, height), pl.ds(column * w, w)


def exchange_kernel(
    nx, ny, columns, forward, backward,
    x_hbm, dy_hbm, samples_hbm, grad_hbm, owners_hbm, left_hbm, right_hbm, lroot_hbm, rroot_hbm,
    *scratch,
):
    names = iter(scratch)

    def several(count):
        return [next(names) for _ in range(count)]

    ahead, home = len(forward), len(backward)
    rows_out = several(home)
    left_out, right_out = several(2)
    mine_rows = several(ahead)
    acc = several(ahead)
    mine = several(ahead)
    pack = several(ahead)
    landing = several(ahead)
    send = several(home)
    back = several(home)
    strips = several(home)
    (held, xs, dys, lroot, rroot, half, direction, left, right,
     x_ref, dy_ref, samples_ref, grad_ref, owners_ref, source_tab, key_tab) = several(16)
    (ready, in_sem, x_send, x_recv, dy_send, dy_recv, keep_sem,
     a_send, a_recv, b_send, b_recv, c_send, c_recv, d_send, d_recv) = several(15)

    me_x, me_y = lax.axis_index("gx"), lax.axis_index("gy")
    fold = nx // ny
    rows = grad_ref.shape[0]
    blk = fold * ny * rows
    w = blk // columns
    br = ny
    tile = BCOL * blk
    dcols = dy_ref.shape[1]
    entries = br * BCOL
    span = SLOTS // GROUPS
    side = math.isqrt(nx)
    up, across = me_x // side, lax.rem(me_x, side)

    def peer_x(d, e):
        return lax.rem(up + d, side) * side + lax.rem(across + e, side)

    def peer_y(d):
        return lax.rem(me_y + d, ny)

    straight = [peer_x(*d) for n in range(1, side) for d in ((n, 0), (0, n))]
    diagonal = [peer_x(m, n) for m in range(1, side) for n in range(1, side)]
    others = [peer_y(n) for n in range(1, ny)]

    def for_straight(act):
        for gx in straight:
            act(gx)

    def for_diagonal(act):
        for gx in diagonal:
            act(gx)

    def for_y(act):
        for gy in others:
            act(gy)

    barrier = pltpu.get_barrier_semaphore()

    def greet(gx, gy):
        pl.semaphore_signal(barrier, inc=1, device_id=(gx, gy), device_id_type=MESH)

    for_straight(lambda gx: greet(gx, me_y))
    for_y(lambda gy: greet(me_x, gy))

    pairs = [
        (samples_hbm, samples_ref), (x_hbm, x_ref), (dy_hbm, dy_ref), (grad_hbm, grad_ref),
        (owners_hbm, owners_ref), (lroot_hbm, lroot), (rroot_hbm, rroot),
        (left_hbm, left), (right_hbm, right),
    ]
    loads = [pltpu.make_async_copy(a, b, in_sem.at[i]) for i, (a, b) in enumerate(pairs)]
    for load in loads[:5]:
        load.start()
    for load in loads[:3]:
        load.wait()
    pool = x_ref.shape[1]
    count = samples_ref.shape[1]
    chosen = (lax.broadcasted_iota(jnp.int32, (pool, count), 0) == samples_ref[...])
    chosen = jnp.where(chosen, 1.0, 0.0).astype(BF16)
    xs[pl.ds(me_x, 1)] = jnp.dot(x_ref[...], chosen, preferred_element_type=F32).astype(BF16)[None]
    dys[pl.ds(me_y, 1)] = lax.dot_general(
        chosen, dy_ref[...], (((0,), (0,)), ((), ())), preferred_element_type=F32
    ).astype(BF16)[None]
    loads[3].wait()

    def narrow(group, _):
        for i, chunk in enumerate(forward):
            column, _, its_rows, _ = cut(chunk, rows, w)
            for block in range(BCOL):
                first = pl.multiple_of(group * tile + block * blk + column * w, 128)
                mine_rows[i][group, block] = grad_ref[its_rows, pl.ds(first, w)].astype(BF16)
        return 0

    lax.fori_loop(0, nx, narrow, 0)

    def send_x(gx):
        pltpu.make_async_remote_copy(
            xs.at[me_x], xs.at[me_x], x_send, x_recv, (gx, me_y), MESH
        ).start()

    def send_dy(gy):
        pltpu.make_async_remote_copy(
            dys.at[me_y], dys.at[me_y], dy_send, dy_recv, (me_x, gy), MESH
        ).start()

    def send_acc(i):
        def act(gx):
            pltpu.make_async_remote_copy(
                mine_rows[i].at[gx], acc[i].at[me_x], a_send.at[i], a_recv.at[i], (gx, me_y), MESH
            ).start()

        return act

    def vouch(d, _):
        pl.semaphore_signal(ready, inc=1, device_id=(peer_x(0, d), me_y), device_id_type=MESH)
        return 0

    pl.semaphore_wait(barrier, 2 * (side - 1) + ny - 1)
    lax.fori_loop(1, side, vouch, 0)
    for_y(send_dy)
    for_straight(send_x)
    for_straight(send_acc(0))
    pl.semaphore_wait(ready, side - 1)
    for_diagonal(send_x)
    for_diagonal(send_acc(0))
    for i in range(ahead):
        pltpu.make_async_copy(mine_rows[i].at[me_x], acc[i].at[me_x], a_recv.at[i]).start()
        if i:
            for_straight(send_acc(i))
            for_diagonal(send_acc(i))

    for load in loads[5:]:
        load.start()

    loads[4].wait()
    keys = []
    owned = jnp.int32(0)
    listed = [owners_ref[e // BCOL, me_x * BCOL + e % BCOL] for e in range(entries)]
    for e in range(entries):
        rank = jnp.int32(0)
        for before in range(e):
            rank = rank + jnp.where(listed[before] == listed[e], 1, 0)
        keys.append(listed[e] * SLOTS + rank)
        key_tab[e] = keys[e]
        owned = owned + jnp.where(listed[e] == me_y, 1, 0)

    def find_source(k, _):
        place = jnp.int32(0)
        for e in range(entries):
            place = place + jnp.where(keys[e] == k, (e % BCOL) * br + e // BCOL, 0)
        source_tab[k] = place
        return 0

    lax.fori_loop(0, ny * SLOTS, find_source, 0)

    def landed(ref, sem):
        pltpu.make_async_copy(ref, ref, sem).wait()

    def picked(first):
        if dcols >= w:
            return dys[first // dcols, :, first % dcols:first % dcols + w]
        return jnp.concatenate([dys[j] for j in range(first // dcols, (first + w) // dcols)], axis=1)

    for i, chunk in enumerate(forward):
        column, height, its_rows, its_columns = cut(chunk, rows, w)
        if i == 0:
            landed(xs.at[pl.ds(0, nx - 1)], x_recv)
            landed(dys.at[pl.ds(0, ny - 1)], dy_recv)
        landed(acc[i], a_recv.at[i])
        for block in range(BCOL):
            product = jnp.dot(
                xs[:, its_rows, :].reshape(nx * height, count),
                picked(block * blk + column * w),
                preferred_element_type=F32,
            ).reshape(nx, height, w)
            total = (acc[i][:, block].astype(F32) + product).astype(BF16)
            mine[i][block * br:(block + 1) * br] = total.reshape(br, fold, height, w)

        def fill(owner, _, i=i):
            for slot in range(SLOTS):
                pack[i][owner, slot] = mine[i][source_tab[owner * SLOTS + slot]]
            return 0

        lax.fori_loop(0, ny, fill, 0)
        for group, k in LEAVE[i]:
            its_slots = pl.ds(group * span, span)
            spot = landing[k].at[me_y, its_slots]
            pltpu.make_async_copy(pack[k].at[me_y, its_slots], spot, b_recv.at[group, k]).start()

            def send_block(gy, group=group, k=k, spot=spot, its_slots=its_slots):
                pltpu.make_async_remote_copy(
                    pack[k].at[gy, its_slots], spot,
                    b_send.at[group, k], b_recv.at[group, k], (me_x, gy), MESH,
                ).start()

            for_y(send_block)

    loads[5].wait()
    loads[6].wait()

    parts = 4
    part = blk // parts
    bands = part // rows

    def from_right(slot, _):
        squares = jnp.zeros((1, blk), F32)
        for p in range(parts):
            product = jnp.dot(
                half[slot, p * part:(p + 1) * part, :], rroot[slot], preferred_element_type=F32
            )
            direction[p * part:(p + 1) * part, :] = product
            squares = squares + jnp.sum(product * product, axis=0, keepdims=True)
        scale = lax.rsqrt(jnp.sum(squares) / (blk * blk) + EPSILON)
        for i, chunk in enumerate(backward):
            column, height, its_rows, its_columns = cut(chunk, rows, w)
            begin = chunk[1] * height
            scaled = (direction[:, its_columns] * scale).astype(BF16).reshape(fold, ny, rows, w)
            for f in range(fold):
                send[i][:, slot, f] = scaled[f, :, begin:begin + height, :]
        return 0

    def statistics(slot, _):
        occupied = slot < owned
        old = jnp.where(occupied, BETA_TWO, 1.0)
        new = jnp.where(occupied, 1.0 - BETA_TWO, 0.0)
        block = held[slot].reshape(blk, blk)
        for p in range(parts):
            at = slice(p * part, (p + 1) * part)
            first = p * bands % ny
            strip = held[slot, p * bands // ny, first:first + bands].reshape(part, blk)
            gram = lax.dot_general(
                strip, block, (((1,), (1,)), ((), ())), preferred_element_type=F32
            )
            left[slot, at, :] = old * left[slot, at, :] + new * gram
            gram = lax.dot_general(
                held[slot, :, :, :, at].reshape(blk, part), block, (((0,), (0,)), ((), ())),
                preferred_element_type=F32,
            )
            right[slot, at, :] = old * right[slot, at, :] + new * gram
        return 0

    def send_back(group, i):
        its_slots = pl.ds(group * span, span)
        spot = back[i].at[pl.ds(me_y * SLOTS + group * span, span)]
        pltpu.make_async_copy(send[i].at[me_y, its_slots], spot, c_recv.at[group, i]).start()

        def act(gy):
            pltpu.make_async_remote_copy(
                send[i].at[gy, its_slots], spot,
                c_send.at[group, i], c_recv.at[group, i], (me_x, gy), MESH,
            ).start()

        for_y(act)

    def sent_back(group, i):
        landed(back[i].at[pl.ds(0, (ny - 1) * span)], c_send.at[group, i])

    for group in range(GROUPS):
        first = group * span
        its_slots = pl.ds(first, span)
        for i, chunk in enumerate(forward):
            _, _, its_rows, its_columns = cut(chunk, rows, w)
            landed(landing[i].at[:, its_slots], b_recv.at[group, i])
            for slot in range(first, first + span):
                for f in range(fold):
                    held[slot, f, :, its_rows, its_columns] = landing[i][:, slot, f]

            def from_left(slot, _, its_columns=its_columns):
                half[slot, :, its_columns] = jnp.dot(
                    lroot[slot], held[slot, :, :, :, its_columns].reshape(blk, w),
                    preferred_element_type=F32,
                ).astype(BF16)
                return 0

            lax.fori_loop(first, first + span, from_left, 0)
        lax.fori_loop(first, first + span, from_right, 0)
        for i in range(FIRST):
            send_back(group, i)
        if group == 0:
            loads[7].wait()
            loads[8].wait()
        lax.fori_loop(first, first + span, statistics, 0)

    for i in range(FIRST, home):
        for group in range(GROUPS):
            send_back(group, i)
    kept = [
        pltpu.make_async_copy(left, left_out, keep_sem.at[0]),
        pltpu.make_async_copy(right, right_out, keep_sem.at[1]),
    ]
    for copy in kept:
        copy.start()

    def for_x(act):
        for_straight(act)
        for_diagonal(act)

    for i in range(home):
        for group in range(GROUPS):
            landed(back[i].at[pl.ds(0, ny * span)], c_recv.at[group, i])
        for e in range(entries):
            r, block = e // BCOL, e % BCOL
            strips[i][r * fold:(r + 1) * fold, block] = back[i][key_tab[e]]
        spot = rows_out[i].at[me_x]
        pltpu.make_async_copy(strips[i].at[me_x], spot, d_recv.at[i]).start()

        def send_rows(gx, i=i, spot=spot):
            pltpu.make_async_remote_copy(
                strips[i].at[gx], spot, d_send.at[i], d_recv.at[i], (gx, me_y), MESH
            ).start()

        for_x(send_rows)

    for i in range(home):
        landed(rows_out[i], d_recv.at[i])
    for i in range(ahead):
        landed(acc[i].at[pl.ds(0, nx - 1)], a_send.at[i])
        for group in range(GROUPS):
            landed(pack[i].at[pl.ds(0, ny - 1), pl.ds(0, span)], b_send.at[group, i])
    for i in range(home):
        for group in range(GROUPS):
            sent_back(group, i)
        landed(strips[i].at[pl.ds(0, nx - 1)], d_send.at[i])
    landed(xs.at[pl.ds(0, nx - 1)], x_send)
    landed(dys.at[pl.ds(0, ny - 1)], dy_send)
    for copy in kept:
        copy.wait()


def finish_kernel(chunks, *refs):
    rows_refs = refs[:len(chunks)]
    left_ref, right_ref, update_out, left_out, right_out, wide, sems, out_sem = refs[len(chunks):]
    copies = [
        pltpu.make_async_copy(left_ref, left_out, sems.at[0]),
        pltpu.make_async_copy(right_ref, right_out, sems.at[1]),
    ]
    for copy in copies:
        copy.start()
    rows = wide.shape[0]
    groups, blocks, _, w = rows_refs[0].shape
    blk = wide.shape[1] // (groups * blocks)
    for group in range(groups):
        for b in range(blocks):
            for ref, chunk in zip(rows_refs, chunks):
                column, height, its_rows, _ = cut(chunk, rows, w)
                at = (group * blocks + b) * blk + column * w
                wide[its_rows, at:at + w] = ref[group, b].astype(F32)
        at = pl.ds(group * blocks * blk, blocks * blk)
        copies.append(pltpu.make_async_copy(wide.at[:, at], update_out.at[:, at], out_sem.at[group]))
        copies[-1].start()
    for copy in copies:
        copy.wait()


def body(
    x_tokens, dy_tokens, samples, grad_acc, owners, left_stats, right_stats, left_roots, right_roots
):
    nx, ny = lax.axis_size("gx"), lax.axis_size("gy")
    rows, cols = grad_acc.shape
    fold = nx // ny
    blk = left_stats.shape[-1]
    w = blk // COLUMNS
    count = samples.shape[0]
    br = ny
    dcols = dy_tokens.shape[1]
    vmem, hbm = pl.BlockSpec(memory_space=pltpu.VMEM), pl.BlockSpec(memory_space=pltpu.HBM)
    anywhere = pl.BlockSpec(memory_space=pl.ANY)

    def each(chunks, *shape):
        heights = [rows // chunk[2] for chunk in chunks]
        return [
            pltpu.VMEM(tuple(h if n is None else n for n in shape), BF16) for h in heights
        ]

    dma = pltpu.SemaphoreType.DMA
    square = (SLOTS, blk, blk)
    *rows_back, new_left, new_right = pl.pallas_call(
        functools.partial(exchange_kernel, nx, ny, COLUMNS, FORWARD, BACKWARD),
        out_shape=(
            *each(BACKWARD, nx, BCOL, None, w),
            pltpu.VMEM(square, F32),
            pltpu.VMEM(square, F32),
        ),
        in_specs=[hbm] * 9,
        out_specs=(anywhere,) * (len(BACKWARD) + 2),
        scratch_shapes=[
            *each(FORWARD, nx, BCOL, None, w),
            *each(FORWARD, nx, BCOL, None, w),
            *each(FORWARD, BCOL * br, fold, None, w),
            *each(FORWARD, ny, SLOTS, fold, None, w),
            *each(FORWARD, ny, SLOTS, fold, None, w),
            *each(BACKWARD, ny, SLOTS, fold, None, w),
            *each(BACKWARD, ny * SLOTS, fold, None, w),
            *each(BACKWARD, nx, BCOL, None, w),
            pltpu.VMEM((SLOTS, fold, ny, rows, blk), BF16),
            pltpu.VMEM((nx, rows, count), BF16),
            pltpu.VMEM((ny, count, dcols), BF16),
            pltpu.VMEM(square, BF16),
            pltpu.VMEM(square, BF16),
            pltpu.VMEM(square, BF16),
            pltpu.VMEM((blk, blk), F32),
            pltpu.VMEM(square, F32),
            pltpu.VMEM(square, F32),
            pltpu.VMEM(x_tokens.shape, BF16),
            pltpu.VMEM(dy_tokens.shape, BF16),
            pltpu.VMEM((1, count), jnp.int32),
            pltpu.VMEM((rows, cols), F32),
            pltpu.SMEM(owners.shape, jnp.int32),
            pltpu.SMEM((ny * SLOTS,), jnp.int32),
            pltpu.SMEM((br * BCOL,), jnp.int32),
            pltpu.SemaphoreType.REGULAR,
            dma((9,)), *[dma] * 4, dma((2,)),
            *[dma((len(FORWARD),))] * 2,
            *[dma((GROUPS, len(FORWARD)))] * 2,
            *[dma((GROUPS, len(BACKWARD)))] * 2,
            *[dma((len(BACKWARD),))] * 2,
        ],
        compiler_params=pltpu.CompilerParams(
            collective_id=0, has_side_effects=True, vmem_limit_bytes=42 * 2**20
        ),
        name="exchange",
    )(*[
        pltpu.with_memory_space_constraint(array, pltpu.HBM)
        for array in (
            x_tokens, dy_tokens, samples.reshape(1, count), grad_acc, owners,
            left_stats[0], right_stats[0], left_roots[0], right_roots[0],
        )
    ])
    update, new_left, new_right = pl.pallas_call(
        functools.partial(finish_kernel, BACKWARD),
        out_shape=(
            jax.ShapeDtypeStruct((rows, cols), F32),
            jax.ShapeDtypeStruct(square, F32),
            jax.ShapeDtypeStruct(square, F32),
        ),
        in_specs=[vmem] * len(BACKWARD) + [anywhere] * 2,
        out_specs=(hbm,) * 3,
        scratch_shapes=[pltpu.VMEM((rows, cols), F32), dma((2,)), dma((nx,))],
        compiler_params=pltpu.CompilerParams(vmem_limit_bytes=12 * 2**20),
        name="finish",
    )(*rows_back, new_left, new_right)
    return update, new_left[None], new_right[None]


def solution(mesh):
    split = P(("gx", "gy"), None)
    deep = P(("gx", "gy"), None, None, None)
    return jax.shard_map(
        body,
        mesh=mesh,
        in_specs=(split, P(None, ("gx", "gy")), P(), split, P(), deep, deep, deep, deep),
        out_specs=(split, deep, deep),
        check_vma=False,
    )
```
